512 devices in a mesh: head: 8 (over z_hi, core), ctx: 64 (over z_lo, y, x).
Axes of the slice: x: 4, y: 8, z: 8 (z_hi: 4, z_lo: 2; z = z_hi * 2 + z_lo), core: 2. Of those that a mesh axis runs over, the one named last changes fastest.
Arguments:
- queries: bfloat16 [8192, 3072], P(('head', 'ctx')), may hold values from -15 to 15
- keys: bfloat16 [8192, 3072], P(('head', 'ctx')), may hold values from -6 to 6
- values: bfloat16 [8192, 3072], P(('head', 'ctx')), may hold values from -6 to 6
- d_queries: bfloat16 [8192, 3072], P(('head', 'ctx')), may hold values from -6 to 6
- d_keys: bfloat16 [8192, 3072], P(('head', 'ctx')), may hold values from -6 to 6
- d_values: bfloat16 [8192, 3072], P(('head', 'ctx')), may hold values from -6 to 6
Outputs:
- attended: bfloat16 [8192, 3072], P(('head', 'ctx'))
- d_attended: bfloat16 [8192, 3072], P(('head', 'ctx'))
The draws below stay inside these ranges and needn't reach their ends.
All inputs are finite; a program needn't handle non-finite values.
Results may differ from the reference program's by a relative error of at most 0.035.
Values may be sent and summed in bfloat16 or wider, within the bound.
A program may use at most 128 MiB of HBM per device.

```python
import jax
import jax.numpy as jnp
from jax import lax

HEADS = 24
HD = 128
SEQ_LEN = 8192


def draw_queries(key, part):
    key = jax.random.fold_in(key, 3)
    sample = jnp.clip(2.5 * jax.random.normal(key, (SEQ_LEN, HEADS * HD), jnp.float32), -15.0, 15.0)
    return sample.astype(jnp.bfloat16)


def draw_keys(key, part):
    key = jax.random.fold_in(key, 5)
    sample = jnp.clip(jax.random.normal(key, (SEQ_LEN, HEADS * HD), jnp.float32), -6.0, 6.0)
    return sample.astype(jnp.bfloat16)


def level_of(key, shape, split, least, top_value):
    factor_of = 1.0
    for axis_at, blocks in split:
        heights = jax.random.uniform(jax.random.fold_in(jax.random.fold_in(key, 6), axis_at), (blocks,), jnp.float32, least / len(split), top_value / len(split))
        factor_of = factor_of * jnp.repeat(jnp.exp(heights), shape[axis_at] // blocks).reshape((-1,) + (1,) * (len(shape) - 1 - axis_at))
    return factor_of


def bell_draw(own_key, shape, scale, reach, cuts=(), dtype=jnp.bfloat16):
    loudness = level_of(own_key, shape, cuts, -0.22, 0.18) if cuts else 1.0
    values = jax.random.normal(own_key, shape, jnp.float32) * scale * loudness
    return jnp.minimum(jnp.maximum(values, -reach), reach).astype(dtype)


def setup_inputs(seed: int = 0) -> dict:
    arg_keys = jax.random.split(jax.random.key(seed), 7)
    queries = draw_queries(jax.random.fold_in(arg_keys[6], 71), 0)
    keys = draw_keys(jax.random.fold_in(arg_keys[6], 71), 0)
    values = bell_draw(arg_keys[2], (SEQ_LEN, HEADS * HD), 1.0, 6.0, ((0, 512),))
    d_queries = bell_draw(arg_keys[3], (SEQ_LEN, HEADS * HD), 1.0, 6.0, ((0, 512),))
    d_keys = bell_draw(arg_keys[4], (SEQ_LEN, HEADS * HD), 1.0, 6.0, ((0, 512),))
    d_values = bell_draw(arg_keys[5], (SEQ_LEN, HEADS * HD), 1.0, 6.0, ((0, 512),))
    return dict(queries=queries, keys=keys, values=values, d_queries=d_queries, d_keys=d_keys, d_values=d_values)


def by_heads(tensor):
    return tensor.reshape(SEQ_LEN, HEADS, HD).transpose(1, 0, 2)


def one_head(head_inputs):
    query_head, key_head, value_head, dquery_head, dkey_head, dvalue_head = head_inputs
    score_scale = HD ** -0.5
    scores = jnp.dot(query_head, key_head.T, preferred_element_type=jnp.float32) * score_scale
    d_scores = (jnp.dot(dquery_head, key_head.T, preferred_element_type=jnp.float32)
                + jnp.dot(query_head, dkey_head.T, preferred_element_type=jnp.float32)) * score_scale
    row_peak = jnp.max(scores, axis=-1, keepdims=True)
    exp_terms = jnp.exp(scores - row_peak)
    weights = exp_terms / jnp.sum(exp_terms, axis=-1, keepdims=True)
    weights_bf = weights.astype(jnp.bfloat16)
    tangent_mix = weights * d_scores
    mix_bf = tangent_mix.astype(jnp.bfloat16)
    row_mean = jnp.sum(tangent_mix, axis=-1, keepdims=True)
    primal = jnp.dot(weights_bf, value_head, preferred_element_type=jnp.float32)
    tangent_out = (jnp.dot(mix_bf, value_head, preferred_element_type=jnp.float32)
                   + jnp.dot(weights_bf, dvalue_head, preferred_element_type=jnp.float32)
                   - primal * row_mean)
    return primal.astype(jnp.bfloat16), tangent_out.astype(jnp.bfloat16)


def reference(queries, keys, values, d_queries, d_keys, d_values):
    inputs = tuple(by_heads(tensor) for tensor in (queries, keys, values, d_queries, d_keys, d_values))
    primal_all, tangent_all = lax.map(one_head, inputs)
    attended = primal_all.transpose(1, 0, 2).reshape(SEQ_LEN, HEADS * HD)
    d_attended = tangent_all.transpose(1, 0, 2).reshape(SEQ_LEN, HEADS * HD)
    return attended, d_attended
```

```python
import functools

import jax
import jax.numpy as jnp
import numpy as np
from jax import lax
from jax.experimental import pallas as pl
from jax.experimental.pallas import tpu as pltpu
from jax.sharding import PartitionSpec as P

HD = 128
CORES = 2
SCALE = HD**-0.5
LOG2E = 1.4426950408889634
MESH = pl.DeviceIdType.MESH

DIMS = (4, 8, 8, 2)

PLANS = ("y", "z", "y")


def head_of(slot, place, dims):
    if slot == 1:
        return 2 * dims[1] + place
    return 2 * place + slot // 2


def steps_of(size):
    half = size // 2
    return {(0, 1): half, (0, -1): size - 1 - half, (1, 1): size - 1 - half, (1, -1): half}


def kernel(
    dims,
    q_ref, k_ref, v_ref, dq_ref, dk_ref, dv_ref,
    out_ref, dout_ref,
    stage, landed, kb, qb, part, stat, rpart, rstat, outgo, outcome, s_buf,
    a_send, a_recv, ring_send, ring_recv, sib_send, sib_recv, q_send, q_recv,
    p_send, p_recv, t_send, t_recv, o_send, o_recv,
):
    nx, ny, nz, zlo = dims
    tok = q_ref.shape[0]
    head, ctx = lax.axis_index("head"), lax.axis_index("ctx")
    core = head % CORES
    z = (head // CORES) * zlo + ctx // (ny * nx)
    y = (ctx // nx) % ny
    x = ctx % nx

    def dev(x, y, z, core):
        return ((z // zlo) * CORES + core, (z % zlo) * (ny * nx) + y * nx + x)

    def a_size(s):
        return ny if PLANS[s] == "y" else nz

    def r_size(s):
        return nz if PLANS[s] == "y" else ny

    def a_me(s):
        return y if PLANS[s] == "y" else z

    def r_me(s):
        return z if PLANS[s] == "y" else y

    def a_dev(s, p):
        return dev(x, p, z, core) if PLANS[s] == "y" else dev(x, y, p, core)

    def r_dev(s, r):
        return dev(x, y, r, core) if PLANS[s] == "y" else dev(x, r, z, core)

    sibling = dev(x, y, z, 1 - core)

    def remote(src, dst, ssem, rsem, to):
        return pltpu.make_async_remote_copy(
            src_ref=src, dst_ref=dst, send_sem=ssem, recv_sem=rsem,
            device_id=to, device_id_type=MESH,
        )

    def drain(ref, sem):
        pltpu.make_async_copy(ref, ref, sem).wait()

    barrier = pltpu.get_barrier_semaphore()
    peers = [sibling]
    peers += [dev(x, (y + d) % ny, z, core) for d in range(1, ny)]
    peers += [dev(x, y, (z + d) % nz, core) for d in range(1, nz)]
    peers += [dev((x + d) % nx, y, z, core) for d in range(1, nx)]
    for peer in peers:
        pl.semaphore_signal(barrier, inc=1, device_id=peer, device_id_type=MESH)

    inputs = (k_ref, dk_ref, v_ref, dv_ref, q_ref, dq_ref)
    for s in range(3):
        for p in range(a_size(s)):
            h = head_of(s, p, dims)
            for i, ref in enumerate(inputs):
                stage[s, p, i] = ref[:, h * HD : (h + 1) * HD]
    pl.semaphore_wait(barrier, len(peers))

    def scatter(s):
        n, me = a_size(s), a_me(s)
        for d in sorted(range(1, n), key=lambda d: -min(d, n - d)):
            p = (me + d) % n
            remote(stage.at[s, p], landed.at[s, me], a_send.at[s], a_recv.at[s], a_dev(s, p)).start()

    def ring_copy(s, piece, way, r, to):
        block = kb.at[s, piece, core, r]
        return remote(block, block, ring_send.at[s, piece], ring_recv.at[s, piece, r], to)

    def sib_copy(s, piece, r):
        block = kb.at[s, piece, core, r]
        return remote(block, block, sib_send.at[s, piece], sib_recv.at[s, piece], sibling)

    def begin(s):
        n, me, r, rn = a_size(s), a_me(s), r_me(s), r_size(s)
        landed[s, me] = stage[s, me]
        if n > 1:
            drain(landed.at[s, pl.ds(0, n - 1)], a_recv.at[s])
        for i in range(4):
            for p in range(n):
                kb[s, i // 2, core, r, i % 2, p * tok : (p + 1) * tok] = landed[s, p, i]
        for piece in range(2):
            for way in (1, -1):
                if steps_of(rn)[piece, way] >= 1:
                    ring_copy(s, piece, way, r, r_dev(s, (r + way) % rn)).start()
        for i in range(2):
            for p in range(n):
                qb[s, x, i, p * tok : (p + 1) * tok] = landed[s, p, 4 + i]
        for d in range(1, nx):
            mine = qb.at[s, x]
            remote(mine, mine, q_send.at[s], q_recv.at[s], dev((x + d) % nx, y, z, core)).start()
        for piece in range(2):
            sib_copy(s, piece, r).start()

    def hop(s, h):
        rn, r = r_size(s), r_me(s)
        for piece in range(2):
            for way in (1, -1):
                most = steps_of(rn)[piece, way]
                if h > most:
                    continue
                at = (r - way * h) % rn
                ring_copy(s, piece, way, at, r_dev(s, r)).wait_recv()
                if h < most:
                    ring_copy(s, piece, way, at, r_dev(s, (r + way) % rn)).start()
                sib_copy(s, piece, at).start()

    def gathered(s):
        rn = r_size(s)
        for piece in range(2):
            drain(kb.at[s, piece, 0, pl.ds(0, rn)], sib_recv.at[s, piece])
        if nx > 1:
            drain(qb.at[s, pl.ds(0, nx - 1)], q_recv.at[s])

    def attend(s, first, count):
        rows = count * 128
        rn = r_size(s)
        keys = CORES * rn * 128

        def pair(ref_at):
            return ref_at.reshape(-1, HD)

        q = pair(qb[s, first : first + count, 0])
        dq = pair(qb[s, first : first + count, 1])
        dq_q = jnp.concatenate([dq, q], axis=1)
        nt = (((1,), (1,)), ((), ()))
        step = 256
        tiles = keys // step

        def block(piece, i, j):
            c, r0 = (2 * j) // rn, (2 * j) % rn
            if rn % 2:
                raise ValueError
            return pair(kb[s, piece, c, r0 : r0 + 2, i])

        peak = None
        for j in range(tiles):
            sc = lax.dot_general(q, block(0, 0, j), nt, preferred_element_type=jnp.float32)
            s_buf[:rows, j * step : (j + 1) * step] = sc
            m = jnp.maximum(sc[:, :128], sc[:, 128:])
            peak = m if peak is None else jnp.maximum(peak, m)
        peak = jnp.max(peak, axis=1, keepdims=True) * (SCALE * LOG2E)
        total = jnp.zeros((rows, 128), jnp.float32)
        mean = jnp.zeros((rows, 128), jnp.float32)
        acc = jnp.zeros((rows, 2 * HD), jnp.float32)
        acc2 = jnp.zeros((rows, HD), jnp.float32)
        for j in range(tiles):
            k, dk, v, dv = block(0, 0, j), block(0, 1, j), block(1, 0, j), block(1, 1, j)
            w = jnp.exp2(s_buf[:rows, j * step : (j + 1) * step] * (SCALE * LOG2E) - peak)
            ds = lax.dot_general(
                dq_q, jnp.concatenate([k, dk], axis=1), nt, preferred_element_type=jnp.float32
            )
            mix = w * ds
            total += w[:, :128] + w[:, 128:]
            mean += mix[:, :128] + mix[:, 128:]
            acc += jnp.dot(
                w.astype(jnp.bfloat16), jnp.concatenate([v, dv], axis=1),
                preferred_element_type=jnp.float32,
            )
            acc2 += jnp.dot(mix.astype(jnp.bfloat16), v, preferred_element_type=jnp.float32)
        total = jnp.sum(total, axis=1, keepdims=True)
        inv = 1.0 / total
        mean = jnp.sum(mean, axis=1, keepdims=True) * (SCALE * inv)
        primal = acc[:, :HD] * inv
        tangent = (acc2 * SCALE + acc[:, HD:]) * inv - primal * mean
        lane = lax.broadcasted_iota(jnp.int32, (128, 128), 1)
        for c in range(count):
            rs = slice(c * 128, (c + 1) * 128)
            part[s, first + c, 0] = primal[rs].astype(jnp.bfloat16)
            part[s, first + c, 1] = tangent[rs].astype(jnp.bfloat16)
            wide = jnp.where(lane == 0, peak[rs], jnp.where(lane == 1, total[rs], mean[rs]))
            stat[s, first + c] = wide.T[:8]

    def share(s):
        for d in range(1, nx):
            to = (x + d) % nx
            dst = dev(to, y, z, core)
            remote(part.at[s, to], rpart.at[s, x], p_send.at[s], p_recv.at[s], dst).start()
            remote(stat.at[s, to], rstat.at[s, x], t_send.at[s], t_recv.at[s], dst).start()

    def merge(s):
        rpart[s, x] = part[s, x]
        rstat[s, x] = stat[s, x]
        if nx > 1:
            drain(rpart.at[s, pl.ds(0, nx - 1)], p_recv.at[s])
            drain(rstat.at[s, pl.ds(0, nx - 1)], t_recv.at[s])
        stats = [rstat[s, i] for i in range(nx)]
        top = functools.reduce(jnp.maximum, [t[0:1] for t in stats])
        shares = [jnp.exp2(t[0:1] - top) * t[1:2] for t in stats]
        inv = 1.0 / functools.reduce(jnp.add, shares)
        shares = [a * inv for a in shares]
        mean = functools.reduce(jnp.add, [a * t[2:3] for a, t in zip(shares, stats)])
        rows = [a for a in shares] + [a * (t[2:3] - mean) for a, t in zip(shares, stats)]
        rows.append(jnp.zeros((128 - len(rows), 128), jnp.float32))
        cols = jnp.concatenate(rows, axis=0).T
        primal = jnp.zeros((128, HD), jnp.float32)
        tangent = jnp.zeros((128, HD), jnp.float32)
        for i in range(nx):
            o = rpart[s, i, 0].astype(jnp.float32)
            primal += cols[:, i : i + 1] * o
            tangent += cols[:, i : i + 1] * rpart[s, i, 1].astype(jnp.float32) + cols[:, nx + i : nx + i + 1] * o
        primal, tangent = primal.astype(jnp.bfloat16), tangent.astype(jnp.bfloat16)
        n, me = a_size(s), a_me(s)
        for p in range(n):
            outgo[s, p, 0] = primal[p * tok : (p + 1) * tok]
            outgo[s, p, 1] = tangent[p * tok : (p + 1) * tok]
        for d in sorted(range(1, n), key=lambda d: -min(d, n - d)):
            p = (me + d) % n
            remote(outgo.at[s, p], outcome.at[s, me], o_send.at[s], o_recv.at[s], a_dev(s, p)).start()
        outcome[s, me] = outgo[s, me]

    def finish(s):
        n = a_size(s)
        if n > 1:
            drain(outcome.at[s, pl.ds(0, n - 1)], o_recv.at[s])
        for p in range(n):
            h = head_of(s, p, dims)
            out_ref[:, h * HD : (h + 1) * HD] = outcome[s, p, 0]
            dout_ref[:, h * HD : (h + 1) * HD] = outcome[s, p, 1]

    for s in range(3):
        scatter(s)
    begin(0)
    begin(1)
    last = [r_size(s) // 2 for s in range(3)]
    for h in range(1, max(last[0], last[1]) + 1):
        if h <= last[0]:
            hop(0, h)
        if h <= last[1]:
            hop(1, h)
        if h == max(last[0] - 1, 1):
            begin(2)

    half = max(nx // 2, 1)
    jobs = []
    for s in range(2):
        jobs.append(functools.partial(gathered, s))
        jobs += [functools.partial(attend, s, f, half) for f in range(0, nx, half)]
        jobs.append(functools.partial(share, s))
    per = -(-len(jobs) // last[2])
    for h in range(1, last[2] + 1):
        for job in jobs[(h - 1) * per : h * per]:
            job()
        hop(2, h)
    merge(0)
    gathered(2)
    for f in range(0, nx, half):
        attend(2, f, half)
    share(2)
    merge(1)
    merge(2)
    for s in range(3):
        finish(s)

    for s in range(3):
        n, rn = a_size(s), r_size(s)
        if n > 1:
            drain(stage.at[s, pl.ds(0, n - 1)], a_send.at[s])
            drain(outgo.at[s, pl.ds(0, n - 1)], o_send.at[s])
        for piece in range(2):
            drain(kb.at[s, piece, 0, pl.ds(0, rn)], sib_send.at[s, piece])
            drain(kb.at[s, piece, 0, pl.ds(0, rn - 1)], ring_send.at[s, piece])
        if nx > 1:
            drain(qb.at[s, pl.ds(0, nx - 1)], q_send.at[s])
            drain(part.at[s, pl.ds(0, nx - 1)], p_send.at[s])
            drain(stat.at[s, pl.ds(0, nx - 1)], t_send.at[s])


def on_device(dims, *arrays):
    nx, ny, nz, _ = dims
    tok = arrays[0].shape[0]
    na = nr = max(ny, nz)
    bf, f32 = jnp.bfloat16, jnp.float32
    dma = pltpu.SemaphoreType.DMA
    shape = jax.ShapeDtypeStruct(arrays[0].shape, bf)
    return pl.pallas_call(
        functools.partial(kernel, dims),
        out_shape=(shape, shape),
        in_specs=[pl.BlockSpec(memory_space=pltpu.VMEM)] * 6,
        out_specs=(pl.BlockSpec(memory_space=pltpu.VMEM),) * 2,
        scratch_shapes=[
            pltpu.VMEM((3, na, 6, tok, HD), bf),
            pltpu.VMEM((3, na, 6, tok, HD), bf),
            pltpu.VMEM((3, 2, CORES, nr, 2, na * tok, HD), bf),
            pltpu.VMEM((3, nx, 2, na * tok, HD), bf),
            pltpu.VMEM((3, nx, 2, 128, HD), bf),
            pltpu.VMEM((3, nx, 8, 128), f32),
            pltpu.VMEM((3, nx, 2, 128, HD), bf),
            pltpu.VMEM((3, nx, 8, 128), f32),
            pltpu.VMEM((3, na, 2, tok, HD), bf),
            pltpu.VMEM((3, na, 2, tok, HD), bf),
            pltpu.VMEM((max(nx // 2, 1) * 128, CORES * nr * 128), f32),
            dma((3,)), dma((3,)),
            dma((3, 2)), dma((3, 2, nr)),
            dma((3, 2)), dma((3, 2)),
            dma((3,)), dma((3,)),
            dma((3,)), dma((3,)),
            dma((3,)), dma((3,)),
            dma((3,)), dma((3,)),
        ],
        compiler_params=pltpu.CompilerParams(
            collective_id=0, has_side_effects=True, vmem_limit_bytes=48 * 1024 * 1024
        ),
        cost_estimate=pl.CostEstimate(flops=5 * 10**9, bytes_accessed=10**6, transcendentals=3 * 10**6),
    )(*arrays)


def solution(mesh):
    spec = P(("head", "ctx"), None)
    return jax.shard_map(
        functools.partial(on_device, DIMS),
        mesh=mesh,
        in_specs=(spec,) * 6,
        out_specs=(spec, spec),
        check_vma=False,
    )
```

```python
import functools

import jax
import jax.numpy as jnp
import numpy as np
from jax import lax
from jax.experimental import pallas as pl
from jax.experimental.pallas import tpu as pltpu
from jax.sharding import PartitionSpec as P

HD = 128
CORES = 2
SCALE = HD**-0.5
LOG2E = 1.4426950408889634
MESH = pl.DeviceIdType.MESH

DIMS = (4, 8, 8, 2)

PLANS = ("y", "z", "y")


def head_of(slot, place, dims):
    if slot == 1:
        return 2 * dims[1] + place
    return 2 * place + slot // 2


def kernel(
    dims,
    q_ref, k_ref, v_ref, dq_ref, dk_ref, dv_ref,
    out_ref, dout_ref,
    loaded, stage, landed, kb, qb, part, stat, rpart, rstat, outgo, outcome, peak_s, total_s, mean_s, acc_s,
    in_sem, a_send, a_recv, ring_send, ring_recv, sib_send, sib_recv, q_send, q_recv,
    p_send, p_recv, t_send, t_recv, o_send, o_recv,
):
    nx, ny, nz, zlo = dims
    tok = q_ref.shape[0]
    head, ctx = lax.axis_index("head"), lax.axis_index("ctx")
    core = head % CORES
    z = (head // CORES) * zlo + ctx // (ny * nx)
    y = (ctx // nx) % ny
    x = ctx % nx

    def dev(x, y, z, core):
        return ((z // zlo) * CORES + core, (z % zlo) * (ny * nx) + y * nx + x)

    def a_size(s):
        return ny if PLANS[s] == "y" else nz

    def r_size(s):
        return nz if PLANS[s] == "y" else ny

    def a_me(s):
        return y if PLANS[s] == "y" else z

    def r_me(s):
        return z if PLANS[s] == "y" else y

    def a_dev(s, p):
        return dev(x, p, z, core) if PLANS[s] == "y" else dev(x, y, p, core)

    def r_dev(s, r):
        return dev(x, y, r, core) if PLANS[s] == "y" else dev(x, r, z, core)

    sibling = dev(x, y, z, 1 - core)
    rows = nx * 128

    def remote(src, dst, ssem, rsem, to):
        return pltpu.make_async_remote_copy(
            src_ref=src, dst_ref=dst, send_sem=ssem, recv_sem=rsem,
            device_id=to, device_id_type=MESH,
        )

    def drain(ref, sem):
        pltpu.make_async_copy(ref, ref, sem).wait()

    inputs = (k_ref, dk_ref, v_ref, dv_ref, q_ref, dq_ref)
    fetches = [pltpu.make_async_copy(ref, loaded.at[i], in_sem.at[i]) for i, ref in enumerate(inputs)]
    for fetch in fetches:
        fetch.start()

    barrier = pltpu.get_barrier_semaphore()
    peers = [sibling]
    peers += [dev(x, (y + d) % ny, z, core) for d in range(1, ny)]
    peers += [dev(x, y, (z + d) % nz, core) for d in range(1, nz)]
    peers += [dev((x + d) % nx, y, z, core) for d in range(1, nx)]
    for peer in peers:
        pl.semaphore_signal(barrier, inc=1, device_id=peer, device_id_type=MESH)

    for fetch in fetches:
        fetch.wait()
    for s in range(3):
        for p in range(a_size(s)):
            h = head_of(s, p, dims)
            for i in range(6):
                stage[s, p, i] = loaded[i, :, h * HD : (h + 1) * HD]
    pl.semaphore_wait(barrier, len(peers))

    parts = (pl.ds(0, 4), pl.ds(4, 2))

    def scatter(s, i):
        n, me = a_size(s), a_me(s)
        for d in sorted(range(1, n), key=lambda d: -min(d, n - d)):
            p = (me + d) % n
            src, dst = stage.at[s, p, parts[i]], landed.at[s, me, parts[i]]
            remote(src, dst, a_send.at[s, i], a_recv.at[s, i], a_dev(s, p)).start()

    def ring_copy(s, way, r, hops, to):
        block, sem = kb.at[s, core, r], ring_recv.at[s, r]
        if hops == r_size(s) // 2:
            block = block.at[pl.ds(0 if way == 1 else 2, 2)]
            sem = sem if way == 1 else ring_recv.at[s, r_size(s)]
        return remote(block, block, ring_send.at[s], sem, to)

    def sib_copy(s, r, h):
        block = kb.at[s, core, r]
        return remote(block, block, sib_send.at[s], sib_recv.at[s, h], sibling)

    def land(s):
        n, me, r = a_size(s), a_me(s), r_me(s)
        landed[s, me] = stage[s, me]
        if n > 1:
            drain(landed.at[s, pl.ds(0, n - 1), parts[0]], a_recv.at[s, 0])
        for i in range(4):
            for p in range(n):
                kb[s, core, r, i, p * tok : (p + 1) * tok] = landed[s, p, i]

    def ask(s):
        n = a_size(s)
        if n > 1:
            drain(landed.at[s, pl.ds(0, n - 1), parts[1]], a_recv.at[s, 1])
        for i in range(2):
            for p in range(n):
                qb[s, x, i, p * tok : (p + 1) * tok] = landed[s, p, 4 + i]
        for d in range(1, nx):
            mine = qb.at[s, x]
            remote(mine, mine, q_send.at[s], q_recv.at[s], dev((x + d) % nx, y, z, core)).start()

    def begin(s):
        rn, r = r_size(s), r_me(s)
        for way in (1, -1):
            ring_copy(s, way, r, 1, r_dev(s, (r + way) % rn)).start()
        sib_copy(s, r, 0).start()

    def hop(s, h):
        rn, r = r_size(s), r_me(s)
        for way in (1, -1):
            at = (r - way * h) % rn
            ring_copy(s, way, at, h, r_dev(s, r)).wait_recv()
            if h < rn // 2:
                ring_copy(s, way, at, h + 1, r_dev(s, (r + way) % rn)).start()
                sib_copy(s, at, h).start()
        if h == rn // 2:
            sib_copy(s, (r + h) % rn, h).start()

    def attend(s, h):
        rn, r = r_size(s), r_me(s)
        places = [(r + h) % rn, (r - h) % rn][: 1 if h in (0, rn // 2) else 2]
        if h == 0 and nx > 1:
            drain(qb.at[s, pl.ds(0, nx - 1)], q_recv.at[s])
        drain(kb.at[s, 0, pl.ds(0, len(places))], sib_recv.at[s, h])

        def block(i):
            return jnp.concatenate([kb[s, c, at, i] for at in places for c in range(CORES)], axis=0)

        k, dk, v, dv = block(0), block(1), block(2), block(3)
        q = qb[s, :, 0].reshape(rows, HD)
        dq = qb[s, :, 1].reshape(rows, HD)
        nt = (((1,), (1,)), ((), ()))
        score = lax.dot_general(q, k, nt, preferred_element_type=jnp.float32)
        d_score = lax.dot_general(
            jnp.concatenate([dq, q], axis=1), jnp.concatenate([k, dk], axis=1), nt,
            preferred_element_type=jnp.float32,
        )
        peak = jnp.max(score, axis=1, keepdims=True) * (SCALE * LOG2E)
        if h:
            old = peak_s[s, :, :1]
            peak = jnp.maximum(peak, old)
            fade = jnp.exp2(old - peak)
        w = jnp.exp2(score * (SCALE * LOG2E) - peak)
        mix = w * d_score

        def lanes(t):
            return functools.reduce(jnp.add, [t[:, i : i + 128] for i in range(0, t.shape[1], 128)])

        total, mean = lanes(w), lanes(mix)
        both = jnp.dot(
            w.astype(jnp.bfloat16), jnp.concatenate([v, dv], axis=1), preferred_element_type=jnp.float32
        )
        mixed = jnp.dot(mix.astype(jnp.bfloat16), v, preferred_element_type=jnp.float32)
        if h:
            total += total_s[s] * fade
            mean += mean_s[s] * fade
            both += acc_s[s, :, : 2 * HD] * fade
            mixed += acc_s[s, :, 2 * HD :] * fade
        if h < rn // 2:
            peak_s[s] = jnp.broadcast_to(peak, (rows, 128))
            total_s[s] = total
            mean_s[s] = mean
            acc_s[s, :, : 2 * HD] = both
            acc_s[s, :, 2 * HD :] = mixed
            return
        total = jnp.sum(total, axis=1, keepdims=True)
        inv = 1.0 / total
        mean = jnp.sum(mean, axis=1, keepdims=True) * (SCALE * inv)
        primal = both[:, :HD] * inv
        tangent = (mixed * SCALE + both[:, HD:]) * inv - primal * mean
        lane = lax.broadcasted_iota(jnp.int32, (128, 128), 1)
        for c in range(nx):
            rs = slice(c * 128, (c + 1) * 128)
            part[s, c, 0] = primal[rs].astype(jnp.bfloat16)
            part[s, c, 1] = tangent[rs].astype(jnp.bfloat16)
            wide = jnp.where(lane == 0, peak[rs], jnp.where(lane == 1, total[rs], mean[rs]))
            stat[s, c] = wide.T[:8]

    def share(s):
        for d in range(1, nx):
            to = (x + d) % nx
            dst = dev(to, y, z, core)
            remote(part.at[s, to], rpart.at[s, x], p_send.at[s], p_recv.at[s], dst).start()
            remote(stat.at[s, to], rstat.at[s, x], t_send.at[s], t_recv.at[s], dst).start()

    def merge(s):
        rpart[s, x] = part[s, x]
        rstat[s, x] = stat[s, x]
        if nx > 1:
            drain(rpart.at[s, pl.ds(0, nx - 1)], p_recv.at[s])
            drain(rstat.at[s, pl.ds(0, nx - 1)], t_recv.at[s])
        stats = [rstat[s, i] for i in range(nx)]
        top = functools.reduce(jnp.maximum, [t[0:1] for t in stats])
        shares = [jnp.exp2(t[0:1] - top) * t[1:2] for t in stats]
        inv = 1.0 / functools.reduce(jnp.add, shares)
        shares = [a * inv for a in shares]
        mean = functools.reduce(jnp.add, [a * t[2:3] for a, t in zip(shares, stats)])
        rows = [a for a in shares] + [a * (t[2:3] - mean) for a, t in zip(shares, stats)]
        rows.append(jnp.zeros((128 - len(rows), 128), jnp.float32))
        cols = jnp.concatenate(rows, axis=0).T
        primal = jnp.zeros((128, HD), jnp.float32)
        tangent = jnp.zeros((128, HD), jnp.float32)
        for i in range(nx):
            o = rpart[s, i, 0].astype(jnp.float32)
            primal += cols[:, i : i + 1] * o
            tangent += cols[:, i : i + 1] * rpart[s, i, 1].astype(jnp.float32) + cols[:, nx + i : nx + i + 1] * o
        primal, tangent = primal.astype(jnp.bfloat16), tangent.astype(jnp.bfloat16)
        n, me = a_size(s), a_me(s)
        for p in range(n):
            outgo[s, p, 0] = primal[p * tok : (p + 1) * tok]
            outgo[s, p, 1] = tangent[p * tok : (p + 1) * tok]
        for d in sorted(range(1, n), key=lambda d: -min(d, n - d)):
            p = (me + d) % n
            remote(outgo.at[s, p], outcome.at[s, me], o_send.at[s], o_recv.at[s], a_dev(s, p)).start()
        outcome[s, me] = outgo[s, me]

    def finish(s):
        n = a_size(s)
        if n > 1:
            drain(outcome.at[s, pl.ds(0, n - 1)], o_recv.at[s])
        for p in range(n):
            h = head_of(s, p, dims)
            out_ref[:, h * HD : (h + 1) * HD] = outcome[s, p, 0]
            dout_ref[:, h * HD : (h + 1) * HD] = outcome[s, p, 1]

    far = r_size(0) // 2
    scatter(0, 0)
    scatter(1, 0)
    scatter(0, 1)
    scatter(1, 1)
    for s in range(2):
        land(s)
        begin(s)
    scatter(2, 0)
    scatter(2, 1)
    ask(0)
    ask(1)
    for h in range(1, far + 1):
        hop(0, h)
        hop(1, h)
        if h == 1:
            land(2)
            begin(2)
            ask(2)
        attend(0, h - 1)
        if h == far:
            attend(0, h)
            share(0)
        if h > 1:
            hop(2, h - 1)
        attend(1, h - 1)
        if h == far:
            attend(1, h)
            share(1)
        if h > 1:
            attend(2, h - 2)
    hop(2, far)
    attend(2, far - 1)
    merge(0)
    attend(2, far)
    share(2)
    merge(1)
    merge(2)
    for s in range(3):
        finish(s)

    for s in range(3):
        n, rn = a_size(s), r_size(s)
        if n > 1:
            for i in range(2):
                drain(stage.at[s, pl.ds(0, n - 1), parts[i]], a_send.at[s, i])
            drain(outgo.at[s, pl.ds(0, n - 1)], o_send.at[s])
        drain(kb.at[s, 0, pl.ds(0, rn)], sib_send.at[s])
        drain(kb.at[s, 0, pl.ds(0, rn - 1)], ring_send.at[s])
        if nx > 1:
            drain(qb.at[s, pl.ds(0, nx - 1)], q_send.at[s])
            drain(part.at[s, pl.ds(0, nx - 1)], p_send.at[s])
            drain(stat.at[s, pl.ds(0, nx - 1)], t_send.at[s])


def on_device(dims, *arrays):
    nx, ny, nz, _ = dims
    tok = arrays[0].shape[0]
    na = nr = max(ny, nz)
    bf, f32 = jnp.bfloat16, jnp.float32
    dma = pltpu.SemaphoreType.DMA
    shape = jax.ShapeDtypeStruct(arrays[0].shape, bf)
    return pl.pallas_call(
        functools.partial(kernel, dims),
        out_shape=(shape, shape),
        in_specs=[pl.BlockSpec(memory_space=pltpu.HBM)] * 6,
        out_specs=(pl.BlockSpec(memory_space=pltpu.VMEM),) * 2,
        scratch_shapes=[
            pltpu.VMEM((6,) + arrays[0].shape, bf),
            pltpu.VMEM((3, na, 6, tok, HD), bf),
            pltpu.VMEM((3, na, 6, tok, HD), bf),
            pltpu.VMEM((3, CORES, nr, 4, na * tok, HD), bf),
            pltpu.VMEM((3, nx, 2, na * tok, HD), bf),
            pltpu.VMEM((3, nx, 2, 128, HD), bf),
            pltpu.VMEM((3, nx, 8, 128), f32),
            pltpu.VMEM((3, nx, 2, 128, HD), bf),
            pltpu.VMEM((3, nx, 8, 128), f32),
            pltpu.VMEM((3, na, 2, tok, HD), bf),
            pltpu.VMEM((3, na, 2, tok, HD), bf),
            pltpu.VMEM((3, nx * 128, 128), f32),
            pltpu.VMEM((3, nx * 128, 128), f32),
            pltpu.VMEM((3, nx * 128, 128), f32),
            pltpu.VMEM((3, nx * 128, 3 * HD), f32),
            dma((6,)),
            dma((3, 2)), dma((3, 2)),
            dma((3,)), dma((3, nr + 1)),
            dma((3,)), dma((3, nr // 2 + 1)),
            dma((3,)), dma((3,)),
            dma((3,)), dma((3,)),
            dma((3,)), dma((3,)),
            dma((3,)), dma((3,)),
        ],
        compiler_params=pltpu.CompilerParams(
            collective_id=0, has_side_effects=True, vmem_limit_bytes=62 * 1024 * 1024
        ),
        cost_estimate=pl.CostEstimate(flops=5 * 10**9, bytes_accessed=10**6, transcendentals=3 * 10**6),
    )(*arrays)


def solution(mesh):
    spec = P(("head", "ctx"), None)
    return jax.shard_map(
        functools.partial(on_device, DIMS),
        mesh=mesh,
        in_specs=(spec,) * 6,
        out_specs=(spec, spec),
        check_vma=False,
    )
```

```python
import functools

import jax
import jax.numpy as jnp
import numpy as np
from jax import lax
from jax.experimental import pallas as pl
from jax.experimental.pallas import tpu as pltpu
from jax.sharding import PartitionSpec as P

HD = 128
CORES = 2
SCALE = HD**-0.5
LOG2E = 1.4426950408889634
MESH = pl.DeviceIdType.MESH

DIMS = (4, 8, 8, 2)

PLANS = ("y", "z", "y")


def head_of(slot, place, dims):
    if slot == 1:
        return 2 * dims[1] + place
    return 2 * place + slot // 2


def kernel(
    dims,
    q_ref, k_ref, v_ref, dq_ref, dk_ref, dv_ref,
    out_ref, dout_ref,
    loaded, stage, landed, kb, qb, part, stat, rpart, rstat, outgo, outcome, peak_s, total_s, mean_s, acc_s,
    in_sem, a_send, a_recv, ring_send, ring_recv, sib_send, sib_recv, q_send, q_recv,
    p_send, p_recv, t_send, t_recv, o_send, o_recv,
):
    nx, ny, nz, zlo = dims
    tok = q_ref.shape[0]
    head, ctx = lax.axis_index("head"), lax.axis_index("ctx")
    core = head % CORES
    z = (head // CORES) * zlo + ctx // (ny * nx)
    y = (ctx // nx) % ny
    x = ctx % nx

    def dev(x, y, z, core):
        return ((z // zlo) * CORES + core, (z % zlo) * (ny * nx) + y * nx + x)

    def a_size(s):
        return ny if PLANS[s] == "y" else nz

    def r_size(s):
        return nz if PLANS[s] == "y" else ny

    def a_me(s):
        return y if PLANS[s] == "y" else z

    def r_me(s):
        return z if PLANS[s] == "y" else y

    def a_dev(s, p):
        return dev(x, p, z, core) if PLANS[s] == "y" else dev(x, y, p, core)

    def r_dev(s, r):
        return dev(x, y, r, core) if PLANS[s] == "y" else dev(x, r, z, core)

    sibling = dev(x, y, z, 1 - core)
    rows = nx * 128

    def remote(src, dst, ssem, rsem, to):
        return pltpu.make_async_remote_copy(
            src_ref=src, dst_ref=dst, send_sem=ssem, recv_sem=rsem,
            device_id=to, device_id_type=MESH,
        )

    def drain(ref, sem):
        pltpu.make_async_copy(ref, ref, sem).wait()

    inputs = (k_ref, dk_ref, v_ref, dv_ref, q_ref, dq_ref)
    fetches = [pltpu.make_async_copy(ref, loaded.at[i], in_sem.at[i]) for i, ref in enumerate(inputs)]
    for fetch in fetches:
        fetch.start()

    barrier = pltpu.get_barrier_semaphore()
    peers = [sibling]
    peers += [dev(x, (y + d) % ny, z, core) for d in range(1, ny)]
    peers += [dev(x, y, (z + d) % nz, core) for d in range(1, nz)]
    peers += [dev((x + d) % nx, y, z, core) for d in range(1, nx)]
    for peer in peers:
        pl.semaphore_signal(barrier, inc=1, device_id=peer, device_id_type=MESH)

    for fetch in fetches:
        fetch.wait()
    for s in range(3):
        for p in range(a_size(s)):
            h = head_of(s, p, dims)
            for i in range(6):
                stage[s, p, i] = loaded[i, :, h * HD : (h + 1) * HD]
    pl.semaphore_wait(barrier, len(peers))

    parts = (pl.ds(0, 4), pl.ds(4, 2))

    def scatter(s, i):
        n, me = a_size(s), a_me(s)
        for d in sorted(range(1, n), key=lambda d: -min(d, n - d)):
            p = (me + d) % n
            src, dst = stage.at[s, p, parts[i]], landed.at[s, me, parts[i]]
            remote(src, dst, a_send.at[s, i], a_recv.at[s, i], a_dev(s, p)).start()

    def ring_copy(s, way, r, hops, to):
        block, sem = kb.at[s, core, r], ring_recv.at[s, r]
        if hops == r_size(s) // 2:
            block = block.at[pl.ds(0 if way == 1 else 2, 2)]
            sem = sem if way == 1 else ring_recv.at[s, r_size(s)]
        return remote(block, block, ring_send.at[s], sem, to)

    def sib_copy(s, r, h):
        block = kb.at[s, core, r]
        return remote(block, block, sib_send.at[s], sib_recv.at[s, h], sibling)

    def land(s):
        n, me, r = a_size(s), a_me(s), r_me(s)
        landed[s, me] = stage[s, me]
        if n > 1:
            drain(landed.at[s, pl.ds(0, n - 1), parts[0]], a_recv.at[s, 0])
        for i in range(4):
            for p in range(n):
                kb[s, core, r, i, p * tok : (p + 1) * tok] = landed[s, p, i]

    def ask(s):
        n = a_size(s)
        if n > 1:
            drain(landed.at[s, pl.ds(0, n - 1), parts[1]], a_recv.at[s, 1])
        for i in range(2):
            for p in range(n):
                qb[s, x, i, p * tok : (p + 1) * tok] = landed[s, p, 4 + i]
        for d in range(1, nx):
            mine = qb.at[s, x]
            remote(mine, mine, q_send.at[s], q_recv.at[s], dev((x + d) % nx, y, z, core)).start()

    def begin(s):
        rn, r = r_size(s), r_me(s)
        for way in (1, -1):
            ring_copy(s, way, r, 1, r_dev(s, (r + way) % rn)).start()
        sib_copy(s, r, 0).start()

    def hop(s, h):
        rn, r = r_size(s), r_me(s)
        for way in (1, -1):
            at = (r - way * h) % rn
            ring_copy(s, way, at, h, r_dev(s, r)).wait_recv()
            if h < rn // 2:
                ring_copy(s, way, at, h + 1, r_dev(s, (r + way) % rn)).start()
                sib_copy(s, at, h).start()
        if h == rn // 2:
            sib_copy(s, (r + h) % rn, h).start()

    def attend(s, h):
        rn, r = r_size(s), r_me(s)
        places = [(r + h) % rn, (r - h) % rn][: 1 if h in (0, rn // 2) else 2]
        if h == 0 and nx > 1:
            drain(qb.at[s, pl.ds(0, nx - 1)], q_recv.at[s])
        drain(kb.at[s, 0, pl.ds(0, len(places))], sib_recv.at[s, h])

        def block(i):
            return jnp.concatenate([kb[s, c, at, i] for at in places for c in range(CORES)], axis=0)

        k, dk, v, dv = block(0), block(1), block(2), block(3)
        q = qb[s, :, 0].reshape(rows, HD)
        dq = qb[s, :, 1].reshape(rows, HD)
        nt = (((1,), (1,)), ((), ()))
        score = lax.dot_general(q, k, nt, preferred_element_type=jnp.float32)
        d_score = lax.dot_general(
            jnp.concatenate([dq, q], axis=1), jnp.concatenate([k, dk], axis=1), nt,
            preferred_element_type=jnp.float32,
        )
        peak = jnp.max(score, axis=1, keepdims=True) * (SCALE * LOG2E)
        if h:
            old = peak_s[s, :, :1]
            peak = jnp.maximum(peak, old)
            fade = jnp.exp2(old - peak)
        w = jnp.exp2(score * (SCALE * LOG2E) - peak)
        mix = w * d_score

        def lanes(t):
            return functools.reduce(jnp.add, [t[:, i : i + 128] for i in range(0, t.shape[1], 128)])

        total, mean = lanes(w), lanes(mix)
        both = jnp.dot(
            w.astype(jnp.bfloat16), jnp.concatenate([v, dv], axis=1), preferred_element_type=jnp.float32
        )
        mixed = jnp.dot(mix.astype(jnp.bfloat16), v, preferred_element_type=jnp.float32)
        if h:
            total += total_s[s] * fade
            mean += mean_s[s] * fade
            both += acc_s[s, :, : 2 * HD] * fade
            mixed += acc_s[s, :, 2 * HD :] * fade
        if h < rn // 2:
            peak_s[s] = jnp.broadcast_to(peak, (rows, 128))
            total_s[s] = total
            mean_s[s] = mean
            acc_s[s, :, : 2 * HD] = both
            acc_s[s, :, 2 * HD :] = mixed
            return
        total = jnp.sum(total, axis=1, keepdims=True)
        inv = 1.0 / total
        mean = jnp.sum(mean, axis=1, keepdims=True) * (SCALE * inv)
        primal = both[:, :HD] * inv
        tangent = (mixed * SCALE + both[:, HD:]) * inv - primal * mean
        lane = lax.broadcasted_iota(jnp.int32, (128, 128), 1)
        for c in range(nx):
            rs = slice(c * 128, (c + 1) * 128)
            part[s, c, 0] = primal[rs].astype(jnp.bfloat16)
            part[s, c, 1] = tangent[rs].astype(jnp.bfloat16)
            wide = jnp.where(lane == 0, peak[rs], jnp.where(lane == 1, total[rs], mean[rs]))
            stat[s, c] = wide.T[:8]

    def share(s):
        for d in range(1, nx):
            to = (x + d) % nx
            dst = dev(to, y, z, core)
            remote(part.at[s, to], rpart.at[s, x], p_send.at[s], p_recv.at[s], dst).start()
            remote(stat.at[s, to], rstat.at[s, x], t_send.at[s], t_recv.at[s], dst).start()

    def merge(s):
        rpart[s, x] = part[s, x]
        rstat[s, x] = stat[s, x]
        if nx > 1:
            drain(rpart.at[s, pl.ds(0, nx - 1)], p_recv.at[s])
            drain(rstat.at[s, pl.ds(0, nx - 1)], t_recv.at[s])
        stats = [rstat[s, i] for i in range(nx)]
        top = functools.reduce(jnp.maximum, [t[0:1] for t in stats])
        shares = [jnp.exp2(t[0:1] - top) * t[1:2] for t in stats]
        inv = 1.0 / functools.reduce(jnp.add, shares)
        shares = [a * inv for a in shares]
        mean = functools.reduce(jnp.add, [a * t[2:3] for a, t in zip(shares, stats)])
        rows = [a for a in shares] + [a * (t[2:3] - mean) for a, t in zip(shares, stats)]
        rows.append(jnp.zeros((128 - len(rows), 128), jnp.float32))
        cols = jnp.concatenate(rows, axis=0).T
        primal = jnp.zeros((128, HD), jnp.float32)
        tangent = jnp.zeros((128, HD), jnp.float32)
        for i in range(nx):
            o = rpart[s, i, 0].astype(jnp.float32)
            primal += cols[:, i : i + 1] * o
            tangent += cols[:, i : i + 1] * rpart[s, i, 1].astype(jnp.float32) + cols[:, nx + i : nx + i + 1] * o
        primal, tangent = primal.astype(jnp.bfloat16), tangent.astype(jnp.bfloat16)
        n, me = a_size(s), a_me(s)
        for p in range(n):
            outgo[s, p, 0] = primal[p * tok : (p + 1) * tok]
            outgo[s, p, 1] = tangent[p * tok : (p + 1) * tok]
        for d in sorted(range(1, n), key=lambda d: -min(d, n - d)):
            p = (me + d) % n
            remote(outgo.at[s, p], outcome.at[s, me], o_send.at[s], o_recv.at[s], a_dev(s, p)).start()
        outcome[s, me] = outgo[s, me]

    def finish(s):
        n = a_size(s)
        if n > 1:
            drain(outcome.at[s, pl.ds(0, n - 1)], o_recv.at[s])
        for p in range(n):
            h = head_of(s, p, dims)
            out_ref[:, h * HD : (h + 1) * HD] = outcome[s, p, 0]
            dout_ref[:, h * HD : (h + 1) * HD] = outcome[s, p, 1]

    far = r_size(0) // 2
    scatter(0, 0)
    scatter(1, 0)
    scatter(0, 1)
    scatter(1, 1)
    for s in range(2):
        land(s)
        begin(s)
    scatter(2, 0)
    scatter(2, 1)
    ask(0)
    ask(1)
    for h in range(1, far + 1):
        hop(0, h)
        hop(1, h)
        if h == 1:
            land(2)
            begin(2)
            ask(2)
        attend(0, h - 1)
        if h == far:
            attend(0, h)
            share(0)
        if h > 1:
            hop(2, h - 1)
        attend(1, h - 1)
        if h == far:
            attend(1, h)
            share(1)
        if h > 1:
            attend(2, h - 2)
    hop(2, far)
    attend(2, far - 1)
    attend(2, far)
    share(2)
    merge(0)
    merge(1)
    merge(2)
    for s in range(3):
        finish(s)

    for s in range(3):
        n, rn = a_size(s), r_size(s)
        if n > 1:
            for i in range(2):
                drain(stage.at[s, pl.ds(0, n - 1), parts[i]], a_send.at[s, i])
            drain(outgo.at[s, pl.ds(0, n - 1)], o_send.at[s])
        drain(kb.at[s, 0, pl.ds(0, rn)], sib_send.at[s])
        drain(kb.at[s, 0, pl.ds(0, rn - 1)], ring_send.at[s])
        if nx > 1:
            drain(qb.at[s, pl.ds(0, nx - 1)], q_send.at[s])
            drain(part.at[s, pl.ds(0, nx - 1)], p_send.at[s])
            drain(stat.at[s, pl.ds(0, nx - 1)], t_send.at[s])


def on_device(dims, *arrays):
    nx, ny, nz, _ = dims
    tok = arrays[0].shape[0]
    na = nr = max(ny, nz)
    bf, f32 = jnp.bfloat16, jnp.float32
    dma = pltpu.SemaphoreType.DMA
    shape = jax.ShapeDtypeStruct(arrays[0].shape, bf)
    return pl.pallas_call(
        functools.partial(kernel, dims),
        out_shape=(shape, shape),
        in_specs=[pl.BlockSpec(memory_space=pltpu.HBM)] * 6,
        out_specs=(pl.BlockSpec(memory_space=pltpu.VMEM),) * 2,
        scratch_shapes=[
            pltpu.VMEM((6,) + arrays[0].shape, bf),
            pltpu.VMEM((3, na, 6, tok, HD), bf),
            pltpu.VMEM((3, na, 6, tok, HD), bf),
            pltpu.VMEM((3, CORES, nr, 4, na * tok, HD), bf),
            pltpu.VMEM((3, nx, 2, na * tok, HD), bf),
            pltpu.VMEM((3, nx, 2, 128, HD), bf),
            pltpu.VMEM((3, nx, 8, 128), f32),
            pltpu.VMEM((3, nx, 2, 128, HD), bf),
            pltpu.VMEM((3, nx, 8, 128), f32),
            pltpu.VMEM((3, na, 2, tok, HD), bf),
            pltpu.VMEM((3, na, 2, tok, HD), bf),
            pltpu.VMEM((3, nx * 128, 128), f32),
            pltpu.VMEM((3, nx * 128, 128), f32),
            pltpu.VMEM((3, nx * 128, 128), f32),
            pltpu.VMEM((3, nx * 128, 3 * HD), f32),
            dma((6,)),
            dma((3, 2)), dma((3, 2)),
            dma((3,)), dma((3, nr + 1)),
            dma((3,)), dma((3, nr // 2 + 1)),
            dma((3,)), dma((3,)),
            dma((3,)), dma((3,)),
            dma((3,)), dma((3,)),
            dma((3,)), dma((3,)),
        ],
        compiler_params=pltpu.CompilerParams(
            collective_id=0, has_side_effects=True, vmem_limit_bytes=40 * 1024 * 1024
        ),
        cost_estimate=pl.CostEstimate(flops=5 * 10**9, bytes_accessed=10**6, transcendentals=3 * 10**6),
    )(*[pltpu.with_memory_space_constraint(array, pltpu.HBM) for array in arrays])


def solution(mesh):
    spec = P(("head", "ctx"), None)
    return jax.shard_map(
        functools.partial(on_device, DIMS),
        mesh=mesh,
        in_specs=(spec,) * 6,
        out_specs=(spec, spec),
        check_vma=False,
    )
```

```python
import functools

import jax
import jax.numpy as jnp
import numpy as np
from jax import lax
from jax.experimental import pallas as pl
from jax.experimental.pallas import tpu as pltpu
from jax.sharding import PartitionSpec as P

HD = 128
CORES = 2
SCALE = HD**-0.5
LOG2E = 1.4426950408889634
MESH = pl.DeviceIdType.MESH

DIMS = (4, 8, 8, 2)

PLANS = ("y", "z", "y")


def head_of(slot, place, dims):
    if slot == 1:
        return 2 * dims[1] + place
    return 2 * place + slot // 2


def kernel(
    dims,
    q_ref, k_ref, v_ref, dq_ref, dk_ref, dv_ref,
    out_ref, dout_ref,
    loaded, stage, landed, kb, qb, part, stat, rpart, rstat, outgo, outcome, peak_s, total_s, mean_s, acc_s,
    in_sem, a_send, a_recv, ring_send, ring_recv, sib_send, sib_recv, q_send, q_recv,
    p_send, p_recv, t_send, t_recv, o_send, o_recv,
):
    nx, ny, nz, zlo = dims
    tok = q_ref.shape[0]
    head, ctx = lax.axis_index("head"), lax.axis_index("ctx")
    core = head % CORES
    z = (head // CORES) * zlo + ctx // (ny * nx)
    y = (ctx // nx) % ny
    x = ctx % nx

    def dev(x, y, z, core):
        return ((z // zlo) * CORES + core, (z % zlo) * (ny * nx) + y * nx + x)

    def a_size(s):
        return ny if PLANS[s] == "y" else nz

    def r_size(s):
        return nz if PLANS[s] == "y" else ny

    def a_me(s):
        return y if PLANS[s] == "y" else z

    def r_me(s):
        return z if PLANS[s] == "y" else y

    def a_dev(s, p):
        return dev(x, p, z, core) if PLANS[s] == "y" else dev(x, y, p, core)

    def r_dev(s, r):
        return dev(x, y, r, core) if PLANS[s] == "y" else dev(x, r, z, core)

    sibling = dev(x, y, z, 1 - core)
    rows = nx * 128

    def remote(src, dst, ssem, rsem, to):
        return pltpu.make_async_remote_copy(
            src_ref=src, dst_ref=dst, send_sem=ssem, recv_sem=rsem,
            device_id=to, device_id_type=MESH,
        )

    def drain(ref, sem):
        pltpu.make_async_copy(ref, ref, sem).wait()

    inputs = (k_ref, dk_ref, v_ref, dv_ref, q_ref, dq_ref)
    fetches = [pltpu.make_async_copy(ref, loaded.at[i], in_sem.at[i]) for i, ref in enumerate(inputs)]
    for fetch in fetches:
        fetch.start()

    barrier = pltpu.get_barrier_semaphore()
    peers = [sibling]
    peers += [dev(x, (y + d) % ny, z, core) for d in range(1, ny)]
    peers += [dev(x, y, (z + d) % nz, core) for d in range(1, nz)]
    peers += [dev((x + d) % nx, y, z, core) for d in range(1, nx)]
    for peer in peers:
        pl.semaphore_signal(barrier, inc=1, device_id=peer, device_id_type=MESH)

    for fetch in fetches:
        fetch.wait()
    for s in range(3):
        for p in range(a_size(s)):
            h = head_of(s, p, dims)
            for i in range(6):
                stage[s, p, i] = loaded[i, :, h * HD : (h + 1) * HD]
    pl.semaphore_wait(barrier, len(peers))

    parts = (pl.ds(0, 4), pl.ds(4, 2))

    def scatter(s, i):
        n, me = a_size(s), a_me(s)
        for d in sorted(range(1, n), key=lambda d: -min(d, n - d)):
            p = (me + d) % n
            src, dst = stage.at[s, p, parts[i]], landed.at[s, me, parts[i]]
            remote(src, dst, a_send.at[s, i], a_recv.at[s, i], a_dev(s, p)).start()

    def ring_copy(s, way, r, hops, to):
        block, sem = kb.at[s, core, r], ring_recv.at[s, r]
        if hops == r_size(s) // 2:
            block = block.at[pl.ds(0 if way == 1 else 2, 2)]
            sem = sem if way == 1 else ring_recv.at[s, r_size(s)]
        return remote(block, block, ring_send.at[s], sem, to)

    def sib_copy(s, r, h):
        block = kb.at[s, core, r]
        return remote(block, block, sib_send.at[s], sib_recv.at[s, h], sibling)

    def land(s):
        n, me, r = a_size(s), a_me(s), r_me(s)
        landed[s, me] = stage[s, me]
        if n > 1:
            drain(landed.at[s, pl.ds(0, n - 1), parts[0]], a_recv.at[s, 0])
        for i in range(4):
            for p in range(n):
                kb[s, core, r, i, p * tok : (p + 1) * tok] = landed[s, p, i]

    def ask(s):
        n = a_size(s)
        if n > 1:
            drain(landed.at[s, pl.ds(0, n - 1), parts[1]], a_recv.at[s, 1])
        for i in range(2):
            for p in range(n):
                qb[s, x, i, p * tok : (p + 1) * tok] = landed[s, p, 4 + i]
        for d in range(1, nx):
            mine = qb.at[s, x]
            remote(mine, mine, q_send.at[s], q_recv.at[s], dev((x + d) % nx, y, z, core)).start()

    def begin(s):
        rn, r = r_size(s), r_me(s)
        for way in (1, -1):
            ring_copy(s, way, r, 1, r_dev(s, (r + way) % rn)).start()
        sib_copy(s, r, 0).start()

    def hop(s, h):
        rn, r = r_size(s), r_me(s)
        if h > rn // 2:
            return
        for way in (1, -1):
            at = (r - way * h) % rn
            ring_copy(s, way, at, h, r_dev(s, r)).wait_recv()
            if h < rn // 2:
                ring_copy(s, way, at, h + 1, r_dev(s, (r + way) % rn)).start()
                sib_copy(s, at, h).start()
        if h == rn // 2:
            sib_copy(s, (r + h) % rn, h).start()

    def attend(s, *levels):
        rn, r = r_size(s), r_me(s)
        places = []
        for h in levels:
            if h > rn // 2:
                continue
            found = [(r + h) % rn, (r - h) % rn][: 1 if h in (0, rn // 2) else 2]
            drain(kb.at[s, 0, pl.ds(0, len(found))], sib_recv.at[s, h])
            places += found
        first, final = 0 in levels, rn // 2 in levels
        if not places:
            return
        if first and nx > 1:
            drain(qb.at[s, pl.ds(0, nx - 1)], q_recv.at[s])

        def block(i):
            return jnp.concatenate([kb[s, c, at, i] for at in places for c in range(CORES)], axis=0)

        k, dk, v, dv = block(0), block(1), block(2), block(3)
        q = qb[s, :, 0].reshape(rows, HD)
        dq = qb[s, :, 1].reshape(rows, HD)
        nt = (((1,), (1,)), ((), ()))
        score = lax.dot_general(q, k, nt, preferred_element_type=jnp.float32)
        d_score = lax.dot_general(
            jnp.concatenate([dq, q], axis=1), jnp.concatenate([k, dk], axis=1), nt,
            preferred_element_type=jnp.float32,
        )
        peak = jnp.max(score, axis=1, keepdims=True) * (SCALE * LOG2E)
        if not first:
            old = peak_s[s, :, :1]
            peak = jnp.maximum(peak, old)
            fade = jnp.exp2(old - peak)
        w = jnp.exp2(score * (SCALE * LOG2E) - peak)
        mix = w * d_score

        def lanes(t):
            return functools.reduce(jnp.add, [t[:, i : i + 128] for i in range(0, t.shape[1], 128)])

        total, mean = lanes(w), lanes(mix)
        both = jnp.dot(
            w.astype(jnp.bfloat16), jnp.concatenate([v, dv], axis=1), preferred_element_type=jnp.float32
        )
        mixed = jnp.dot(mix.astype(jnp.bfloat16), v, preferred_element_type=jnp.float32)
        if not first:
            total += total_s[s] * fade
            mean += mean_s[s] * fade
            both += acc_s[s, :, : 2 * HD] * fade
            mixed += acc_s[s, :, 2 * HD :] * fade
        if not final:
            peak_s[s] = jnp.broadcast_to(peak, (rows, 128))
            total_s[s] = total
            mean_s[s] = mean
            acc_s[s, :, : 2 * HD] = both
            acc_s[s, :, 2 * HD :] = mixed
            return
        total = jnp.sum(total, axis=1, keepdims=True)
        inv = 1.0 / total
        mean = jnp.sum(mean, axis=1, keepdims=True) * (SCALE * inv)
        primal = both[:, :HD] * inv
        tangent = (mixed * SCALE + both[:, HD:]) * inv - primal * mean
        lane = lax.broadcasted_iota(jnp.int32, (128, 128), 1)
        for c in range(nx):
            rs = slice(c * 128, (c + 1) * 128)
            part[s, c, 0] = primal[rs].astype(jnp.bfloat16)
            part[s, c, 1] = tangent[rs].astype(jnp.bfloat16)
            wide = jnp.where(lane == 0, peak[rs], jnp.where(lane == 1, total[rs], mean[rs]))
            stat[s, c] = wide.T[:8]

    def share(s):
        for d in range(1, nx):
            to = (x + d) % nx
            dst = dev(to, y, z, core)
            remote(part.at[s, to], rpart.at[s, x], p_send.at[s], p_recv.at[s], dst).start()
            remote(stat.at[s, to], rstat.at[s, x], t_send.at[s], t_recv.at[s], dst).start()

    def merge(s):
        rpart[s, x] = part[s, x]
        rstat[s, x] = stat[s, x]
        if nx > 1:
            drain(rpart.at[s, pl.ds(0, nx - 1)], p_recv.at[s])
            drain(rstat.at[s, pl.ds(0, nx - 1)], t_recv.at[s])
        stats = [rstat[s, i] for i in range(nx)]
        top = functools.reduce(jnp.maximum, [t[0:1] for t in stats])
        shares = [jnp.exp2(t[0:1] - top) * t[1:2] for t in stats]
        inv = 1.0 / functools.reduce(jnp.add, shares)
        shares = [a * inv for a in shares]
        mean = functools.reduce(jnp.add, [a * t[2:3] for a, t in zip(shares, stats)])
        rows = [a for a in shares] + [a * (t[2:3] - mean) for a, t in zip(shares, stats)]
        rows.append(jnp.zeros((128 - len(rows), 128), jnp.float32))
        cols = jnp.concatenate(rows, axis=0).T
        primal = jnp.zeros((128, HD), jnp.float32)
        tangent = jnp.zeros((128, HD), jnp.float32)
        for i in range(nx):
            o = rpart[s, i, 0].astype(jnp.float32)
            primal += cols[:, i : i + 1] * o
            tangent += cols[:, i : i + 1] * rpart[s, i, 1].astype(jnp.float32) + cols[:, nx + i : nx + i + 1] * o
        primal, tangent = primal.astype(jnp.bfloat16), tangent.astype(jnp.bfloat16)
        n, me = a_size(s), a_me(s)
        for p in range(n):
            outgo[s, p, 0] = primal[p * tok : (p + 1) * tok]
            outgo[s, p, 1] = tangent[p * tok : (p + 1) * tok]
        for d in sorted(range(1, n), key=lambda d: -min(d, n - d)):
            p = (me + d) % n
            remote(outgo.at[s, p], outcome.at[s, me], o_send.at[s], o_recv.at[s], a_dev(s, p)).start()
        outcome[s, me] = outgo[s, me]

    def finish(s):
        n = a_size(s)
        if n > 1:
            drain(outcome.at[s, pl.ds(0, n - 1)], o_recv.at[s])
        for p in range(n):
            h = head_of(s, p, dims)
            out_ref[:, h * HD : (h + 1) * HD] = outcome[s, p, 0]
            dout_ref[:, h * HD : (h + 1) * HD] = outcome[s, p, 1]

    scatter(0, 0)
    scatter(1, 0)
    scatter(0, 1)
    scatter(1, 1)
    land(0)
    begin(0)
    land(1)
    begin(1)
    scatter(2, 0)
    scatter(2, 1)
    ask(0)
    ask(1)
    hop(0, 1)
    hop(1, 1)
    land(2)
    begin(2)
    ask(2)
    hop(0, 2)
    hop(1, 2)
    hop(2, 1)
    attend(0, 0, 1)
    attend(1, 0, 1)
    hop(0, 3)
    hop(1, 3)
    hop(2, 2)
    attend(0, 2)
    attend(1, 2)
    attend(2, 0, 1)
    hop(0, 4)
    hop(1, 4)
    hop(2, 3)
    attend(0, 3, 4)
    share(0)
    attend(1, 3, 4)
    share(1)
    attend(2, 2)
    attend(2, 3)
    hop(2, 4)
    attend(2, 4)
    share(2)
    merge(0)
    merge(1)
    merge(2)
    for s in range(3):
        finish(s)

    for s in range(3):
        n, rn = a_size(s), r_size(s)
        if n > 1:
            for i in range(2):
                drain(stage.at[s, pl.ds(0, n - 1), parts[i]], a_send.at[s, i])
            drain(outgo.at[s, pl.ds(0, n - 1)], o_send.at[s])
        drain(kb.at[s, 0, pl.ds(0, rn)], sib_send.at[s])
        drain(kb.at[s, 0, pl.ds(0, rn - 1)], ring_send.at[s])
        if nx > 1:
            drain(qb.at[s, pl.ds(0, nx - 1)], q_send.at[s])
            drain(part.at[s, pl.ds(0, nx - 1)], p_send.at[s])
            drain(stat.at[s, pl.ds(0, nx - 1)], t_send.at[s])


def on_device(dims, *arrays):
    nx, ny, nz, _ = dims
    tok = arrays[0].shape[0]
    na = nr = max(ny, nz)
    bf, f32 = jnp.bfloat16, jnp.float32
    dma = pltpu.SemaphoreType.DMA
    shape = jax.ShapeDtypeStruct(arrays[0].shape, bf)
    return pl.pallas_call(
        functools.partial(kernel, dims),
        out_shape=(shape, shape),
        in_specs=[pl.BlockSpec(memory_space=pltpu.HBM)] * 6,
        out_specs=(pl.BlockSpec(memory_space=pltpu.VMEM),) * 2,
        scratch_shapes=[
            pltpu.VMEM((6,) + arrays[0].shape, bf),
            pltpu.VMEM((3, na, 6, tok, HD), bf),
            pltpu.VMEM((3, na, 6, tok, HD), bf),
            pltpu.VMEM((3, CORES, nr, 4, na * tok, HD), bf),
            pltpu.VMEM((3, nx, 2, na * tok, HD), bf),
            pltpu.VMEM((3, nx, 2, 128, HD), bf),
            pltpu.VMEM((3, nx, 8, 128), f32),
            pltpu.VMEM((3, nx, 2, 128, HD), bf),
            pltpu.VMEM((3, nx, 8, 128), f32),
            pltpu.VMEM((3, na, 2, tok, HD), bf),
            pltpu.VMEM((3, na, 2, tok, HD), bf),
            pltpu.VMEM((3, nx * 128, 128), f32),
            pltpu.VMEM((3, nx * 128, 128), f32),
            pltpu.VMEM((3, nx * 128, 128), f32),
            pltpu.VMEM((3, nx * 128, 3 * HD), f32),
            dma((6,)),
            dma((3, 2)), dma((3, 2)),
            dma((3,)), dma((3, nr + 1)),
            dma((3,)), dma((3, nr // 2 + 1)),
            dma((3,)), dma((3,)),
            dma((3,)), dma((3,)),
            dma((3,)), dma((3,)),
            dma((3,)), dma((3,)),
        ],
        compiler_params=pltpu.CompilerParams(
            collective_id=0, has_side_effects=True, vmem_limit_bytes=40 * 1024 * 1024
        ),
        cost_estimate=pl.CostEstimate(flops=5 * 10**9, bytes_accessed=10**6, transcendentals=3 * 10**6),
    )(*[pltpu.with_memory_space_constraint(array, pltpu.HBM) for array in arrays])


def solution(mesh):
    spec = P(("head", "ctx"), None)
    return jax.shard_map(
        functools.partial(on_device, DIMS),
        mesh=mesh,
        in_specs=(spec,) * 6,
        out_specs=(spec, spec),
        check_vma=False,
    )
```

```python
import functools

import jax
import jax.numpy as jnp
import numpy as np
from jax import lax
from jax.experimental import pallas as pl
from jax.experimental.pallas import tpu as pltpu
from jax.sharding import PartitionSpec as P

HD = 128
CORES = 2
SCALE = HD**-0.5
LOG2E = 1.4426950408889634
MESH = pl.DeviceIdType.MESH

DIMS = (4, 8, 8, 2)

PLANS = ("y", "z", "y")


def head_of(slot, place, dims):
    if slot == 1:
        return 2 * dims[1] + place
    return 2 * place + slot // 2


def kernel(
    dims,
    q_ref, k_ref, v_ref, dq_ref, dk_ref, dv_ref,
    out_ref, dout_ref,
    loaded, stage, landed, kb, qb, part, stat, rpart, rstat, outgo, outcome, peak_s, total_s, mean_s, acc_s,
    in_sem, a_send, a_recv, ring_send, ring_recv, sib_send, sib_recv, q_send, q_recv,
    p_send, p_recv, t_send, t_recv, o_send, o_recv,
):
    nx, ny, nz, zlo = dims
    tok = q_ref.shape[0]
    head, ctx = lax.axis_index("head"), lax.axis_index("ctx")
    core = head % CORES
    z = (head // CORES) * zlo + ctx // (ny * nx)
    y = (ctx // nx) % ny
    x = ctx % nx

    def dev(x, y, z, core):
        return ((z // zlo) * CORES + core, (z % zlo) * (ny * nx) + y * nx + x)

    def a_size(s):
        return ny if PLANS[s] == "y" else nz

    def r_size(s):
        return nz if PLANS[s] == "y" else ny

    def a_me(s):
        return y if PLANS[s] == "y" else z

    def r_me(s):
        return z if PLANS[s] == "y" else y

    def a_dev(s, p):
        return dev(x, p, z, core) if PLANS[s] == "y" else dev(x, y, p, core)

    def r_dev(s, r):
        return dev(x, y, r, core) if PLANS[s] == "y" else dev(x, r, z, core)

    sibling = dev(x, y, z, 1 - core)
    rows = nx * 128

    def remote(src, dst, ssem, rsem, to):
        return pltpu.make_async_remote_copy(
            src_ref=src, dst_ref=dst, send_sem=ssem, recv_sem=rsem,
            device_id=to, device_id_type=MESH,
        )

    def drain(ref, sem):
        pltpu.make_async_copy(ref, ref, sem).wait()

    inputs = (k_ref, dk_ref, v_ref, dv_ref, q_ref, dq_ref)
    fetches = [pltpu.make_async_copy(ref, loaded.at[i], in_sem.at[i]) for i, ref in enumerate(inputs)]
    for fetch in fetches:
        fetch.start()

    barrier = pltpu.get_barrier_semaphore()
    peers = [sibling]
    peers += [dev(x, (y + d) % ny, z, core) for d in range(1, ny)]
    peers += [dev(x, y, (z + d) % nz, core) for d in range(1, nz)]
    peers += [dev((x + d) % nx, y, z, core) for d in range(1, nx)]
    for peer in peers:
        pl.semaphore_signal(barrier, inc=1, device_id=peer, device_id_type=MESH)

    for fetch in fetches:
        fetch.wait()
    for s in range(3):
        for p in range(a_size(s)):
            h = head_of(s, p, dims)
            for i in range(6):
                stage[s, p, i] = loaded[i, :, h * HD : (h + 1) * HD]
    pl.semaphore_wait(barrier, len(peers))

    parts = (pl.ds(0, 4), pl.ds(4, 2))

    def scatter(s, i):
        n, me = a_size(s), a_me(s)
        for d in sorted(range(1, n), key=lambda d: -min(d, n - d)):
            p = (me + d) % n
            src, dst = stage.at[s, p, parts[i]], landed.at[s, me, parts[i]]
            remote(src, dst, a_send.at[s, i], a_recv.at[s, i], a_dev(s, p)).start()

    def ring_copy(s, way, r, hops, to):
        block, sem = kb.at[s, core, r], ring_recv.at[s, r]
        if hops == r_size(s) // 2:
            block = block.at[pl.ds(0 if way == 1 else 2, 2)]
            sem = sem if way == 1 else ring_recv.at[s, r_size(s)]
        return remote(block, block, ring_send.at[s], sem, to)

    def sib_copy(s, r, h):
        block = kb.at[s, core, r]
        return remote(block, block, sib_send.at[s], sib_recv.at[s, h], sibling)

    def land(s):
        n, me, r = a_size(s), a_me(s), r_me(s)
        landed[s, me] = stage[s, me]
        if n > 1:
            drain(landed.at[s, pl.ds(0, n - 1), parts[0]], a_recv.at[s, 0])
        for i in range(4):
            for p in range(n):
                kb[s, core, r, i, p * tok : (p + 1) * tok] = landed[s, p, i]

    def ask(s):
        n = a_size(s)
        if n > 1:
            drain(landed.at[s, pl.ds(0, n - 1), parts[1]], a_recv.at[s, 1])
        for i in range(2):
            for p in range(n):
                qb[s, x, i, p * tok : (p + 1) * tok] = landed[s, p, 4 + i]
        for d in range(1, nx):
            mine = qb.at[s, x]
            remote(mine, mine, q_send.at[s], q_recv.at[s], dev((x + d) % nx, y, z, core)).start()

    def begin(s):
        rn, r = r_size(s), r_me(s)
        for way in (1, -1):
            ring_copy(s, way, r, 1, r_dev(s, (r + way) % rn)).start()
        sib_copy(s, r, 0).start()

    def hop(s, h):
        rn, r = r_size(s), r_me(s)
        if h > rn // 2:
            return
        for way in (1, -1):
            at = (r - way * h) % rn
            ring_copy(s, way, at, h, r_dev(s, r)).wait_recv()
            if h < rn // 2:
                ring_copy(s, way, at, h + 1, r_dev(s, (r + way) % rn)).start()
                sib_copy(s, at, h).start()
        if h == rn // 2:
            sib_copy(s, (r + h) % rn, h).start()

    def attend(s, *levels):
        rn, r = r_size(s), r_me(s)
        places = []
        for h in levels:
            if h > rn // 2:
                continue
            found = [(r + h) % rn, (r - h) % rn][: 1 if h in (0, rn // 2) else 2]
            drain(kb.at[s, 0, pl.ds(0, len(found))], sib_recv.at[s, h])
            places += found
        first, final = 0 in levels, rn // 2 in levels
        if not places:
            return
        if first and nx > 1:
            drain(qb.at[s, pl.ds(0, nx - 1)], q_recv.at[s])

        def block(i):
            return jnp.concatenate([kb[s, c, at, i] for at in places for c in range(CORES)], axis=0)

        k, dk, v, dv = block(0), block(1), block(2), block(3)
        q = qb[s, :, 0].reshape(rows, HD)
        dq = qb[s, :, 1].reshape(rows, HD)
        nt = (((1,), (1,)), ((), ()))
        score = lax.dot_general(q, k, nt, preferred_element_type=jnp.float32)
        d_score = lax.dot_general(
            jnp.concatenate([dq, q], axis=1), jnp.concatenate([k, dk], axis=1), nt,
            preferred_element_type=jnp.float32,
        )
        peak = jnp.max(score, axis=1, keepdims=True) * (SCALE * LOG2E)
        if not first:
            old = peak_s[s, :, :1]
            peak = jnp.maximum(peak, old)
            fade = jnp.exp2(old - peak)
        w = jnp.exp2(score * (SCALE * LOG2E) - peak)
        mix = w * d_score

        def lanes(t):
            return functools.reduce(jnp.add, [t[:, i : i + 128] for i in range(0, t.shape[1], 128)])

        total, mean = lanes(w), lanes(mix)
        both = jnp.dot(
            w.astype(jnp.bfloat16), jnp.concatenate([v, dv], axis=1), preferred_element_type=jnp.float32
        )
        mixed = jnp.dot(mix.astype(jnp.bfloat16), v, preferred_element_type=jnp.float32)
        if not first:
            total += total_s[s] * fade
            mean += mean_s[s] * fade
            both += acc_s[s, :, : 2 * HD] * fade
            mixed += acc_s[s, :, 2 * HD :] * fade
        if not final:
            peak_s[s] = jnp.broadcast_to(peak, (rows, 128))
            total_s[s] = total
            mean_s[s] = mean
            acc_s[s, :, : 2 * HD] = both
            acc_s[s, :, 2 * HD :] = mixed
            return
        total = jnp.sum(total, axis=1, keepdims=True)
        inv = 1.0 / total
        mean = jnp.sum(mean, axis=1, keepdims=True) * (SCALE * inv)
        primal = both[:, :HD] * inv
        tangent = (mixed * SCALE + both[:, HD:]) * inv - primal * mean
        lane = lax.broadcasted_iota(jnp.int32, (128, 128), 1)
        for c in range(nx):
            rs = slice(c * 128, (c + 1) * 128)
            part[s, c, 0] = primal[rs].astype(jnp.bfloat16)
            part[s, c, 1] = tangent[rs].astype(jnp.bfloat16)
            wide = jnp.where(lane == 0, peak[rs], jnp.where(lane == 1, total[rs], mean[rs]))
            stat[s, c] = wide.T[:8]

    def share(s):
        for d in sorted(range(1, nx), key=lambda d: -min(d, nx - d)):
            to = (x + d) % nx
            dst = dev(to, y, z, core)
            remote(stat.at[s, to], rstat.at[s, x], t_send.at[s], t_recv.at[s], dst).start()
            remote(part.at[s, to], rpart.at[s, x], p_send.at[s], p_recv.at[s], dst).start()

    def merge(s):
        rpart[s, x] = part[s, x]
        rstat[s, x] = stat[s, x]
        if nx > 1:
            drain(rpart.at[s, pl.ds(0, nx - 1)], p_recv.at[s])
            drain(rstat.at[s, pl.ds(0, nx - 1)], t_recv.at[s])
        stats = [rstat[s, i] for i in range(nx)]
        top = functools.reduce(jnp.maximum, [t[0:1] for t in stats])
        shares = [jnp.exp2(t[0:1] - top) * t[1:2] for t in stats]
        inv = 1.0 / functools.reduce(jnp.add, shares)
        shares = [a * inv for a in shares]
        mean = functools.reduce(jnp.add, [a * t[2:3] for a, t in zip(shares, stats)])
        rows = [a for a in shares] + [a * (t[2:3] - mean) for a, t in zip(shares, stats)]
        rows.append(jnp.zeros((128 - len(rows), 128), jnp.float32))
        cols = jnp.concatenate(rows, axis=0).T
        primal = jnp.zeros((128, HD), jnp.float32)
        tangent = jnp.zeros((128, HD), jnp.float32)
        for i in range(nx):
            o = rpart[s, i, 0].astype(jnp.float32)
            primal += cols[:, i : i + 1] * o
            tangent += cols[:, i : i + 1] * rpart[s, i, 1].astype(jnp.float32) + cols[:, nx + i : nx + i + 1] * o
        primal, tangent = primal.astype(jnp.bfloat16), tangent.astype(jnp.bfloat16)
        n, me = a_size(s), a_me(s)
        for p in range(n):
            outgo[s, p, 0] = primal[p * tok : (p + 1) * tok]
            outgo[s, p, 1] = tangent[p * tok : (p + 1) * tok]
        for d in sorted(range(1, n), key=lambda d: -min(d, n - d)):
            p = (me + d) % n
            remote(outgo.at[s, p], outcome.at[s, me], o_send.at[s], o_recv.at[s], a_dev(s, p)).start()
        outcome[s, me] = outgo[s, me]

    def finish(s):
        n = a_size(s)
        if n > 1:
            drain(outcome.at[s, pl.ds(0, n - 1)], o_recv.at[s])
        for p in range(n):
            h = head_of(s, p, dims)
            out_ref[:, h * HD : (h + 1) * HD] = outcome[s, p, 0]
            dout_ref[:, h * HD : (h + 1) * HD] = outcome[s, p, 1]

    scatter(0, 0)
    scatter(1, 0)
    scatter(0, 1)
    scatter(1, 1)
    land(0)
    begin(0)
    land(1)
    begin(1)
    scatter(2, 0)
    scatter(2, 1)
    ask(0)
    ask(1)
    hop(0, 1)
    hop(1, 1)
    land(2)
    begin(2)
    ask(2)
    hop(0, 2)
    hop(1, 2)
    hop(2, 1)
    attend(0, 0, 1)
    attend(1, 0, 1)
    hop(0, 3)
    hop(1, 3)
    hop(2, 2)
    attend(0, 2)
    attend(1, 2)
    attend(2, 0, 1)
    hop(0, 4)
    hop(1, 4)
    hop(2, 3)
    attend(0, 3, 4)
    share(0)
    attend(1, 3, 4)
    share(1)
    attend(2, 2)
    attend(2, 3)
    hop(2, 4)
    attend(2, 4)
    share(2)
    merge(0)
    merge(1)
    merge(2)
    for s in range(3):
        finish(s)

    for s in range(3):
        n, rn = a_size(s), r_size(s)
        if n > 1:
            for i in range(2):
                drain(stage.at[s, pl.ds(0, n - 1), parts[i]], a_send.at[s, i])
            drain(outgo.at[s, pl.ds(0, n - 1)], o_send.at[s])
        drain(kb.at[s, 0, pl.ds(0, rn)], sib_send.at[s])
        drain(kb.at[s, 0, pl.ds(0, rn - 1)], ring_send.at[s])
        if nx > 1:
            drain(qb.at[s, pl.ds(0, nx - 1)], q_send.at[s])
            drain(part.at[s, pl.ds(0, nx - 1)], p_send.at[s])
            drain(stat.at[s, pl.ds(0, nx - 1)], t_send.at[s])


def on_device(dims, *arrays):
    nx, ny, nz, _ = dims
    tok = arrays[0].shape[0]
    na = nr = max(ny, nz)
    bf, f32 = jnp.bfloat16, jnp.float32
    dma = pltpu.SemaphoreType.DMA
    shape = jax.ShapeDtypeStruct(arrays[0].shape, bf)
    return pl.pallas_call(
        functools.partial(kernel, dims),
        out_shape=(shape, shape),
        in_specs=[pl.BlockSpec(memory_space=pltpu.HBM)] * 6,
        out_specs=(pl.BlockSpec(memory_space=pltpu.VMEM),) * 2,
        scratch_shapes=[
            pltpu.VMEM((6,) + arrays[0].shape, bf),
            pltpu.VMEM((3, na, 6, tok, HD), bf),
            pltpu.VMEM((3, na, 6, tok, HD), bf),
            pltpu.VMEM((3, CORES, nr, 4, na * tok, HD), bf),
            pltpu.VMEM((3, nx, 2, na * tok, HD), bf),
            pltpu.VMEM((3, nx, 2, 128, HD), bf),
            pltpu.VMEM((3, nx, 8, 128), f32),
            pltpu.VMEM((3, nx, 2, 128, HD), bf),
            pltpu.VMEM((3, nx, 8, 128), f32),
            pltpu.VMEM((3, na, 2, tok, HD), bf),
            pltpu.VMEM((3, na, 2, tok, HD), bf),
            pltpu.VMEM((3, nx * 128, 128), f32),
            pltpu.VMEM((3, nx * 128, 128), f32),
            pltpu.VMEM((3, nx * 128, 128), f32),
            pltpu.VMEM((3, nx * 128, 3 * HD), f32),
            dma((6,)),
            dma((3, 2)), dma((3, 2)),
            dma((3,)), dma((3, nr + 1)),
            dma((3,)), dma((3, nr // 2 + 1)),
            dma((3,)), dma((3,)),
            dma((3,)), dma((3,)),
            dma((3,)), dma((3,)),
            dma((3,)), dma((3,)),
        ],
        compiler_params=pltpu.CompilerParams(
            collective_id=0, has_side_effects=True, vmem_limit_bytes=40 * 1024 * 1024
        ),
        cost_estimate=pl.CostEstimate(flops=5 * 10**9, bytes_accessed=10**6, transcendentals=3 * 10**6),
    )(*[pltpu.with_memory_space_constraint(array, pltpu.HBM) for array in arrays])


def solution(mesh):
    spec = P(("head", "ctx"), None)
    return jax.shard_map(
        functools.partial(on_device, DIMS),
        mesh=mesh,
        in_specs=(spec,) * 6,
        out_specs=(spec, spec),
        check_vma=False,
    )
```
